32 devices in a mesh: groups: 2 (over y), rows: 4 (over z), tm: 2 (over x), dp: 2 (over core).
Axes of the slice: x: 2, y: 2, z: 4, core: 2. Of those that a mesh axis runs over, the one named last changes fastest.
Arguments:
- frames_in: bfloat16 [4, 4, 16, 320, 128], P(('groups', 'dp'), 'tm', 'rows'), parts along dimension 0, may hold values from -6 to 6
- gain: float32 [128], replicated, may hold values from 0.5 to 1.5
- spatial_w: bfloat16 [3, 3, 128, 128], replicated, may hold values from -0.1875 to 0.1875
- temporal_w: bfloat16 [3, 128, 128], replicated, may hold values from -0.3125 to 0.3125
- cotangent: bfloat16 [4, 4, 16, 320, 128], P(('groups', 'dp'), 'tm', 'rows'), parts along dimension 0, may hold values from -6 to 6
Outputs:
- block_out: bfloat16 [4, 4, 16, 320, 128], P(('groups', 'dp'), 'tm', 'rows'), parts along dimension 0
- grad_input: bfloat16 [4, 4, 16, 320, 128], P(('groups', 'dp'), 'tm', 'rows'), parts along dimension 0
- grad_spatial: float32 [6, 3, 128, 128], P('groups'), parts along dimension 0
- grad_temporal: float32 [6, 128, 128], P('groups'), parts along dimension 0
- grad_gain: float32 [256], P('groups'), parts along dimension 0
The draws below stay inside these ranges and needn't reach their ends.
There are 2 independent parts, one for each index of `groups`. The reference program is written for one: setup_inputs(seed, part) draws one part's arguments, and reference() takes and returns one part's arrays. A program takes and returns all parts, laid end to end along the dimension named above; an argument that names none is the same for every part. Nothing has to cross between parts.
All inputs are finite; a program needn't handle non-finite values.
Results may differ from the reference program's by a relative error of at most 0.0054.
Values may be sent and summed in bfloat16 or wider, within the bound.
A program may use at most 64 MiB of HBM per device.

```python
import jax
import jax.numpy as jnp
from jax import lax

C = 128
WID = 320
CLIPS = 2
FRAMES = 4
HEIGHT = 16


def block_scale(key, extent, cuts, least, top_value):
    def one(dim, shards_of):
        heights = jax.random.uniform(jax.random.fold_in(jax.random.fold_in(key, 6), dim), (shards_of,), jnp.float32, least / len(cuts), top_value / len(cuts))
        return jnp.repeat(jnp.exp(heights), extent[dim] // shards_of).reshape((-1,) + (1,) * (len(extent) - dim - 1))

    loudness = one(*cuts[0])
    for cut in cuts[1:]:
        loudness = loudness * one(*cut)
    return loudness


def centred(key, dims, spread, bound, split=(), dtype=jnp.bfloat16):
    drawn = spread * jax.random.normal(key, dims, jnp.float32)
    if split:
        drawn = drawn * block_scale(key, dims, split, -0.22, 0.18)
    return jnp.clip(drawn, -bound, bound).astype(dtype)


def setup_inputs(seed: int = 0, part: int = 0) -> dict:
    keys = jax.random.split(jax.random.key(seed), 6)
    own_keys = jax.random.split(jax.random.fold_in(keys[5], part), 6)
    return {
        "frames_in": centred(own_keys[0], (CLIPS, FRAMES, HEIGHT, WID, C), 1.0, 6.0, ((0, 2), (1, 2), (2, 4))),
        "gain": jnp.clip(jax.random.uniform(keys[1], (C,), jnp.float32, 0.5, 1.5), 0.5, 1.5),
        "spatial_w": centred(keys[2], (3, 3, C, C), (9 * C) ** -0.5, 0.1875),
        "temporal_w": centred(keys[3], (3, C, C), (3 * C) ** -0.5, 0.3125),
        "cotangent": centred(own_keys[4], (CLIPS, FRAMES, HEIGHT, WID, C), 1.0, 6.0, ((0, 2), (1, 2), (2, 4))),
    }


EPS = 1e-06
HIGH = lax.Precision.HIGHEST

def flat_f32(block):
    return block.reshape(-1, block.shape[-1]).astype(jnp.float32)

def product(left, right):
    return jnp.dot(flat_f32(left), right.astype(jnp.float32), precision=HIGH)

def outer_sum(left, right):
    return jnp.einsum('nc,nd->cd', flat_f32(left), flat_f32(right), precision=HIGH)

def reference(frames_in, gain, spatial_w, temporal_w, cotangent):
    clips, frames, height, width, chans = frames_in.shape
    lead = (clips, frames, height, width, chans)
    upper = frames_in.astype(jnp.float32)
    recip = lax.rsqrt(lax.optimization_barrier(jnp.mean(upper * upper, axis=-1, keepdims=True)) + EPS)
    unit = upper * recip
    normed = (unit * gain).astype(jnp.bfloat16)
    padded = jnp.pad(normed, ((0, 0), (0, 0), (1, 1), (1, 1), (0, 0)))
    hidden = jnp.zeros((clips * frames * height * width, chans), jnp.float32)
    for i in range(3):
        for j in range(3):
            hidden = hidden + product(padded[:, :, i:i + height, j:j + width], spatial_w[i, j])
    hidden = hidden.reshape(lead)
    act = jax.nn.silu(hidden).astype(jnp.bfloat16)
    act_pad = jnp.pad(act, ((0, 0), (2, 0), (0, 0), (0, 0), (0, 0)))
    mixed = jnp.zeros((clips * frames * height * width, chans), jnp.float32)
    for k in range(3):
        mixed = mixed + product(act_pad[:, 2 - k:2 - k + frames], temporal_w[k])
    block_out = (upper + mixed.reshape(lead)).astype(jnp.bfloat16)
    cot_pad = jnp.pad(cotangent, ((0, 0), (0, 2), (0, 0), (0, 0), (0, 0)))
    dact = jnp.zeros((clips * frames * height * width, chans), jnp.float32)
    for k in range(3):
        dact = dact + product(cot_pad[:, k:k + frames], temporal_w[k].T)
    sig = jax.nn.sigmoid(hidden)
    dhid = (dact.reshape(lead) * sig * (1.0 + hidden * (1.0 - sig))).astype(jnp.bfloat16)
    dpad = jnp.pad(dhid, ((0, 0), (0, 0), (1, 1), (1, 1), (0, 0)))
    dnorm = jnp.zeros((clips * frames * height * width, chans), jnp.float32)
    for i in range(3):
        for j in range(3):
            dnorm = dnorm + product(dpad[:, :, 2 - i:2 - i + height, 2 - j:2 - j + width], spatial_w[i, j].T)
    dnorm = dnorm.reshape(lead)
    scale = 1.0 / float(clips * frames * height * width) ** 0.5
    spatial_rows = []
    for i in range(3):
        spatial_cols = []
        for j in range(3):
            spatial_cols.append(outer_sum(padded[:, :, i:i + height, j:j + width], dhid))
        spatial_rows.append(jnp.stack(spatial_cols))
    grad_spatial = jnp.stack(spatial_rows) * scale
    grad_temporal = jnp.stack([outer_sum(act_pad[:, 2 - k:2 - k + frames], cotangent) for k in range(3)]) * scale
    grad_gain = lax.optimization_barrier(jnp.sum(dnorm * unit, axis=(0, 1, 2, 3))) * scale
    dunit = dnorm * gain
    grad_input = (cotangent.astype(jnp.float32) + recip * (dunit - unit * lax.optimization_barrier(jnp.mean(dunit * unit, axis=-1, keepdims=True)))).astype(jnp.bfloat16)
    return (block_out, grad_input, grad_spatial, grad_temporal, grad_gain)
```

```python
import functools
import math

import jax
import jax.numpy as jnp
from jax import lax
from jax.experimental import pallas as pl
from jax.experimental.pallas import tpu as pltpu
from jax.sharding import PartitionSpec as P

EPS = 1e-06
MESH = pl.DeviceIdType.MESH
F32 = jnp.float32
BF16 = jnp.bfloat16


def dot(a, b):
    return lax.dot_general(a, b, (((1,), (0,)), ((), ())), preferred_element_type=F32)


def dot_nt(a, b):
    return lax.dot_general(a, b, (((1,), (1,)), ((), ())), preferred_element_type=F32)


def kernel(
    sizes,
    scale,
    u_ref,
    gain_ref,
    ws_ref,
    wt_ref,
    cot_ref,
    out_ref,
    gin_ref,
    gs_ref,
    gt_ref,
    gg_ref,
    wsr,
    wtr,
    xs,
    xst,
    hid,
    act,
    actt,
    d3,
    nsend,
    nrecv,
    dsend,
    drecv,
    cotn,
    actp,
    g32,
    g16,
    rdp,
    s16,
    rbuf,
    r16,
    nss,
    nrs,
    dss,
    drs,
    css,
    crs,
    ass,
    ars,
    e1,
    rss,
    rrs,
    gss,
    grs,
    fss,
    frs,
):
    rows, tms, n, ch = sizes
    F, H, W, C = u_ref.shape
    C3 = 3 * C
    half = n * ch
    z = lax.axis_index("rows")
    t = lax.axis_index("tm")
    d = lax.axis_index("dp")
    p = t * rows + z

    def peer(o):
        q = lax.rem(p + o, n)
        return q, {"tm": q // rows, "rows": lax.rem(q, rows)}

    barrier = pltpu.get_barrier_semaphore()
    for o in range(1, n):
        pl.semaphore_signal(barrier, inc=1, device_id=peer(o)[1], device_id_type=MESH)
    partner = {"dp": 1 - d}
    pl.semaphore_signal(barrier, inc=1, device_id=partner, device_id_type=MESH)
    pl.semaphore_wait(barrier, n)

    def rcopy(src, dst, ss, rs, dev):
        return pltpu.make_async_remote_copy(
            src_ref=src, dst_ref=dst, send_sem=ss, recv_sem=rs, device_id=dev, device_id_type=MESH
        )

    order = [0, H - 1] + list(range(1, H - 1))
    inner = list(range(1, H - 1)) + [0, H - 1]

    def cot_copy(h):
        return rcopy(cot_ref.at[:, h], cotn.at[:, h], css.at[h], crs.at[h], {"tm": t - 1})

    def act_copy(h):
        return rcopy(act.at[:, h], actp.at[:, h], ass.at[h], ars.at[h], {"tm": t + 1})

    def n_copy(s):
        return rcopy(nsend.at[s], nrecv.at[s], nss.at[s], nrs.at[s], {"rows": z - 1 + 2 * s})

    def d_copy(s):
        return rcopy(dsend.at[s], drecv.at[s], dss.at[s], drs.at[s], {"rows": z - 1 + 2 * s})

    def has(s):
        return z > 0 if s == 0 else z < rows - 1

    @pl.when(t > 0)
    def _():
        for h in order:
            cot_copy(h).start()

    sub = lax.broadcasted_iota(jnp.int32, (W, C), 0)

    def shifted(x):
        before = jnp.where(sub == 0, 0.0, pltpu.roll(x, 1, 0))
        after = jnp.where(sub == W - 1, 0.0, pltpu.roll(x, W - 1, 0))
        return before, after

    def put_x(f, slot, x):
        before, after = shifted(x)
        for j, part in enumerate((before, x, after)):
            xs[f, slot, :, j * C : (j + 1) * C] = part.astype(BF16)
            xst[f, slot, j * C : (j + 1) * C, :] = part.T.astype(BF16)

    def put_d(f, slot, x):
        before, after = shifted(x)
        for j, part in enumerate((after, x, before)):
            d3[f, slot, :, j * C : (j + 1) * C] = part.astype(BF16)

    gain = gain_ref[...]

    def norm(f, h):
        u = u_ref[f, h].astype(F32)
        r = lax.rsqrt(jnp.mean(u * u, axis=-1, keepdims=True) + EPS)
        return r, u * r

    def each_frame(fn):
        def body(f, carry):
            fn(f)
            return carry

        lax.fori_loop(0, F, body, 0)

    for h in order:

        def fn(f, h=h):
            x = (norm(f, h)[1] * gain).astype(BF16)
            if h == 0:
                nsend[0, f] = x
            if h == H - 1:
                nsend[1, f] = x
            put_x(f, h + 1, x.astype(F32))

        each_frame(fn)
        if h == 0:

            @pl.when(has(0))
            def _():
                n_copy(0).start()

        if h == H - 1:

            @pl.when(has(1))
            def _():
                n_copy(1).start()

    for i in range(3):
        for j in range(3):
            wsr[i, :, j * C : (j + 1) * C] = ws_ref[i, j * C : (j + 1) * C, :]
    for k in range(3):
        wtr[:, k * C : (k + 1) * C] = wt_ref[k * C : (k + 1) * C, :]

    def halo(s, copy, recv, put):
        slot = H + 1 if s == 0 else 0

        @pl.when(has(1 - s))
        def _():
            copy(s).wait_recv()
            each_frame(lambda f: put(f, slot, recv[s, f].astype(F32)))

        @pl.when(jnp.logical_not(has(1 - s)))
        def _():
            each_frame(lambda f: put(f, slot, jnp.zeros((W, C), F32)))

    for h in inner:
        if h == 0:
            halo(1, n_copy, nrecv, put_x)
        if h == H - 1:
            halo(0, n_copy, nrecv, put_x)

        def fn(f, h=h):
            v = dot(xs[f, h], ws_ref[0]) + dot(xs[f, h + 1], ws_ref[1]) + dot(xs[f, h + 2], ws_ref[2])
            hid[f, h] = v
            a = v * jax.nn.sigmoid(v)
            act[f, h] = a.astype(BF16)
            actt[f, h] = a.T.astype(BF16)

        each_frame(fn)

        @pl.when(t < tms - 1)
        def _():
            act_copy(h).start()

    @pl.when(t == tms - 1)
    def _():
        cotn[...] = jnp.zeros_like(cotn)

    g32[...] = jnp.zeros_like(g32)
    for h in order:

        @pl.when(t < tms - 1)
        def _():
            cot_copy(h).wait_recv()

        cots = [cot_ref[f, h] for f in range(F)] + [cotn[f, h] for f in range(F)]
        tsum = None
        for f in range(F):
            cc = jnp.concatenate(cots[f : f + 3], axis=-1)
            dact = dot_nt(cc, wtr[...])
            v = hid[f, h]
            s = jax.nn.sigmoid(v)
            dh = (dact * s * (1.0 + v * (1.0 - s))).astype(BF16)
            if h == 0:
                dsend[0, f] = dh
            if h == H - 1:
                dsend[1, f] = dh
            put_d(f, h + 1, dh.astype(F32))
            term = dot(actt[f, h], cc)
            tsum = term if tsum is None else tsum + term
        if h == 0:

            @pl.when(has(0))
            def _():
                d_copy(0).start()

        if h == H - 1:

            @pl.when(has(1))
            def _():
                d_copy(1).start()

        for k in range(3):
            g32[3 * C3 + k * C : 3 * C3 + (k + 1) * C, :] += tsum[:, k * C : (k + 1) * C]
        for i in range(3):
            total = None
            for f in range(F):
                term = dot(xst[f, h + i], d3[f, h + 1, :, C : 2 * C])
                total = term if total is None else total + term
            g32[i * C3 : (i + 1) * C3, :] += total

    g16[...] = g32[...].astype(BF16)
    own = pl.multiple_of(d * half, 16)
    other = pl.multiple_of((1 - d) * half, 16)
    swap = rcopy(g16.at[pl.ds(other, half)], rdp, e1.at[0], e1.at[1], partner)
    swap.start()

    def back(f, h):
        dn = (
            dot_nt(d3[f, h + 2], wsr[0])
            + dot_nt(d3[f, h + 1], wsr[1])
            + dot_nt(d3[f, h], wsr[2])
        )
        r, unit = norm(f, h)
        du = dn * gain
        gin_ref[f, h] = (
            cot_ref[f, h].astype(F32)
            + r * (du - unit * jnp.mean(du * unit, axis=-1, keepdims=True))
        ).astype(BF16)

    swap.wait()
    g32[pl.ds(own, half), :] = g32[pl.ds(own, half), :] + rdp[...].astype(F32)
    s16[...] = g32[pl.ds(own, half), :].astype(BF16)

    def scatter(o):
        q, dev = peer(o)
        return rcopy(
            s16.at[pl.ds(pl.multiple_of(q * ch, 16), ch)],
            rbuf.at[o - 1],
            rss.at[o - 1],
            rrs.at[o - 1],
            dev,
        )

    for o in range(1, n):
        scatter(o).start()

    for h in range(1, H - 1):
        each_frame(functools.partial(back, h=h))

    total = g32[pl.ds(pl.multiple_of(own + p * ch, 8), ch), :]
    for o in range(1, n):
        scatter(o).wait_recv()
        total = total + rbuf[o - 1].astype(F32)

    def place(dd, q):
        return pl.ds(pl.multiple_of((dd * n + q) * ch, 16), ch)

    r16[place(d, p), :] = total.astype(BF16)

    def gather(o):
        return rcopy(r16.at[place(d, p)], r16.at[place(d, p)], gss.at[o - 1], grs.at[o - 1], peer(o)[1])

    def forward(o):
        ref = r16.at[place(d, lax.rem(p - o + n, n))]
        return rcopy(ref, ref, fss.at[o], frs.at[o], partner)

    for o in range(1, n):
        gather(o).start()
    forward(0).start()

    halo(1, d_copy, drecv, put_d)
    each_frame(functools.partial(back, h=0))
    halo(0, d_copy, drecv, put_d)
    each_frame(functools.partial(back, h=H - 1))

    @pl.when(t == 0)
    def _():
        actp[...] = jnp.zeros_like(actp)

    for o in range(1, n):
        gather(o).wait_recv()
        forward(o).start()

    for h in inner:

        @pl.when(t > 0)
        def _():
            act_copy(h).wait_recv()

        acts = [actp[f, h] for f in range(F)] + [act[f, h] for f in range(F)]
        for f in range(F):
            cc = jnp.concatenate([acts[F + f], acts[F + f - 1], acts[F + f - 2]], axis=-1)
            out_ref[f, h] = (u_ref[f, h].astype(F32) + dot(cc, wt_ref[...])).astype(BF16)

    for o in range(n):
        forward(o).wait_recv()
    total = None
    for b in range(9):
        g = r16[b * C : (b + 1) * C, :].astype(F32) * scale
        gs_ref[b] = g
        term = g * ws_ref[b // 3, (b % 3) * C : (b % 3 + 1) * C, :].astype(F32)
        total = term if total is None else total + term
    gg_ref[...] = jnp.sum(total.T, axis=0, keepdims=True) / gain
    for k in range(3):
        gt_ref[k] = r16[(9 + k) * C : (10 + k) * C, :].astype(F32) * scale

    for o in range(1, n):
        scatter(o).wait_send()
        gather(o).wait_send()
    for o in range(n):
        forward(o).wait_send()
    for s in range(2):

        @pl.when(has(s))
        def _():
            n_copy(s).wait_send()
            d_copy(s).wait_send()

    @pl.when(t > 0)
    def _():
        for h in range(H):
            cot_copy(h).wait_send()

    @pl.when(t < tms - 1)
    def _():
        for h in range(H):
            act_copy(h).wait_send()


def shards(frames_in, gain, spatial_w, temporal_w, cotangent):
    _, F, H, W, C = frames_in.shape
    rows, tms, dps = lax.axis_size("rows"), lax.axis_size("tm"), lax.axis_size("dp")
    n = rows * tms
    ch = -(-12 * C // (dps * n * 16)) * 16
    total = dps * n * ch
    scale = 1.0 / math.sqrt(F * H * W * n * dps)
    shape = (F, H, W, C)
    vmem = pl.BlockSpec(memory_space=pltpu.VMEM)
    dma = pltpu.SemaphoreType.DMA
    out = pl.pallas_call(
        functools.partial(kernel, (rows, tms, n, ch), scale),
        out_shape=(
            jax.ShapeDtypeStruct(shape, BF16),
            jax.ShapeDtypeStruct(shape, BF16),
            jax.ShapeDtypeStruct((9, C, C), F32),
            jax.ShapeDtypeStruct((3, C, C), F32),
            jax.ShapeDtypeStruct((1, C), F32),
        ),
        in_specs=[vmem] * 5,
        out_specs=(vmem,) * 5,
        scratch_shapes=[
            pltpu.VMEM((3, C, 3 * C), BF16),
            pltpu.VMEM((C, 3 * C), BF16),
            pltpu.VMEM((F, H + 2, W, 3 * C), BF16),
            pltpu.VMEM((F, H + 2, 3 * C, W), BF16),
            pltpu.VMEM(shape, F32),
            pltpu.VMEM(shape, BF16),
            pltpu.VMEM((F, H, C, W), BF16),
            pltpu.VMEM((F, H + 2, W, 3 * C), BF16),
            pltpu.VMEM((2, F, W, C), BF16),
            pltpu.VMEM((2, F, W, C), BF16),
            pltpu.VMEM((2, F, W, C), BF16),
            pltpu.VMEM((2, F, W, C), BF16),
            pltpu.VMEM(shape, BF16),
            pltpu.VMEM(shape, BF16),
            pltpu.VMEM((total, C), F32),
            pltpu.VMEM((total, C), BF16),
            pltpu.VMEM((n * ch, C), BF16),
            pltpu.VMEM((n * ch, C), BF16),
            pltpu.VMEM((n - 1, ch, C), BF16),
            pltpu.VMEM((total, C), BF16),
            dma((2,)),
            dma((2,)),
            dma((2,)),
            dma((2,)),
            dma((H,)),
            dma((H,)),
            dma((H,)),
            dma((H,)),
            dma((2,)),
            dma((n - 1,)),
            dma((n - 1,)),
            dma((n - 1,)),
            dma((n - 1,)),
            dma((n,)),
            dma((n,)),
        ],
        compiler_params=pltpu.CompilerParams(
            collective_id=0, has_side_effects=True, vmem_limit_bytes=48 * 1024 * 1024
        ),
    )(
        frames_in.reshape(shape),
        gain.reshape(1, C),
        spatial_w.reshape(3, 3 * C, C),
        temporal_w.reshape(3 * C, C),
        cotangent.reshape(shape),
    )
    block_out, grad_input, gs, gt, gg = out
    return (
        block_out.reshape(frames_in.shape),
        grad_input.reshape(frames_in.shape),
        gs.reshape(3, 3, C, C),
        gt,
        gg.reshape(C),
    )


def solution(mesh):
    split = P(("groups", "dp"), "tm", "rows", None, None)
    return jax.shard_map(
        shards,
        mesh=mesh,
        in_specs=(split, P(), P(), P(), split),
        out_specs=(split, split, P("groups", None, None, None), P("groups", None, None), P("groups")),
        check_vma=False,
    )
```

```python
import functools
import math

import jax
import jax.numpy as jnp
from jax import lax
from jax.experimental import pallas as pl
from jax.experimental.pallas import tpu as pltpu
from jax.sharding import PartitionSpec as P

EPS = 1e-06
MESH = pl.DeviceIdType.MESH
F32 = jnp.float32
BF16 = jnp.bfloat16


def dot(a, b):
    return lax.dot_general(a, b, (((1,), (0,)), ((), ())), preferred_element_type=F32)


def dot_nt(a, b):
    return lax.dot_general(a, b, (((1,), (1,)), ((), ())), preferred_element_type=F32)


def kernel(
    sizes,
    scale,
    u_in,
    gain_ref,
    ws_in,
    wt_in,
    cot_in,
    out_hbm,
    gin_hbm,
    gs_ref,
    gt_ref,
    gg_ref,
    u_ref,
    ws_ref,
    wt_ref,
    cot_ref,
    lsem,
    out_ref,
    gin_ref,
    osem,
    wsr,
    wtr,
    xs,
    xst,
    hid,
    act,
    actt,
    d3,
    nsend,
    nrecv,
    dsend,
    drecv,
    cotn,
    actp,
    g32,
    g16,
    rdp,
    s16,
    rbuf,
    r16,
    nss,
    nrs,
    dss,
    drs,
    css,
    crs,
    ass,
    ars,
    e1,
    rss,
    rrs,
    gss,
    grs,
    fss,
    frs,
):
    rows, tms, n, ch = sizes
    F, H, W, C = u_ref.shape
    loads = [
        pltpu.make_async_copy(a, b, lsem.at[i])
        for i, (a, b) in enumerate(
            ((u_in, u_ref), (ws_in, ws_ref), (cot_in, cot_ref), (wt_in, wt_ref))
        )
    ]
    for load in loads:
        load.start()
    C3 = 3 * C
    half = n * ch
    z = lax.axis_index("rows")
    t = lax.axis_index("tm")
    d = lax.axis_index("dp")
    p = t * rows + z

    def peer(o):
        q = lax.rem(p + o, n)
        return q, {"tm": q // rows, "rows": lax.rem(q, rows)}

    barrier = pltpu.get_barrier_semaphore()
    for o in range(1, n):
        pl.semaphore_signal(barrier, inc=1, device_id=peer(o)[1], device_id_type=MESH)
    partner = {"dp": 1 - d}
    pl.semaphore_signal(barrier, inc=1, device_id=partner, device_id_type=MESH)
    pl.semaphore_wait(barrier, n)

    def rcopy(src, dst, ss, rs, dev):
        return pltpu.make_async_remote_copy(
            src_ref=src, dst_ref=dst, send_sem=ss, recv_sem=rs, device_id=dev, device_id_type=MESH
        )

    order = [0, H - 1] + list(range(1, H - 1))
    inner = list(range(1, H - 1)) + [0, H - 1]

    def cot_copy(h):
        return rcopy(cot_in.at[:, h], cotn.at[:, h], css.at[h], crs.at[h], {"tm": t - 1})

    def act_copy(h):
        return rcopy(act.at[:, h], actp.at[:, h], ass.at[h], ars.at[h], {"tm": t + 1})

    def n_copy(s):
        return rcopy(nsend.at[s], nrecv.at[s], nss.at[s], nrs.at[s], {"rows": z - 1 + 2 * s})

    def d_copy(s):
        return rcopy(dsend.at[s], drecv.at[s], dss.at[s], drs.at[s], {"rows": z - 1 + 2 * s})

    def has(s):
        return z > 0 if s == 0 else z < rows - 1

    @pl.when(t > 0)
    def _():
        for h in order:
            cot_copy(h).start()

    sub = lax.broadcasted_iota(jnp.int32, (W, C), 0)

    def shifted(x):
        before = jnp.where(sub == 0, 0.0, pltpu.roll(x, 1, 0))
        after = jnp.where(sub == W - 1, 0.0, pltpu.roll(x, W - 1, 0))
        return before, after

    def put_x(f, slot, x):
        before, after = shifted(x)
        for j, part in enumerate((before, x, after)):
            xs[f, slot, :, j * C : (j + 1) * C] = part.astype(BF16)
            xst[f, slot, j * C : (j + 1) * C, :] = part.T.astype(BF16)

    def put_d(f, slot, x):
        before, after = shifted(x)
        for j, part in enumerate((after, x, before)):
            d3[f, slot, :, j * C : (j + 1) * C] = part.astype(BF16)

    gain = gain_ref[...]
    loads[0].wait()

    def norm(f, h):
        u = u_ref[f, h].astype(F32)
        r = lax.rsqrt(jnp.mean(u * u, axis=-1, keepdims=True) + EPS)
        return r, u * r

    def each_frame(fn):
        def body(f, carry):
            fn(f)
            return carry

        lax.fori_loop(0, F, body, 0)

    for h in order:

        def fn(f, h=h):
            x = (norm(f, h)[1] * gain).astype(BF16)
            if h == 0:
                nsend[0, f] = x
            if h == H - 1:
                nsend[1, f] = x
            put_x(f, h + 1, x.astype(F32))

        each_frame(fn)
        if h == 0:

            @pl.when(has(0))
            def _():
                n_copy(0).start()

        if h == H - 1:

            @pl.when(has(1))
            def _():
                n_copy(1).start()

    for load in loads[1:]:
        load.wait()
    for i in range(3):
        for j in range(3):
            wsr[i, :, j * C : (j + 1) * C] = ws_ref[i, j * C : (j + 1) * C, :]
    for k in range(3):
        wtr[:, k * C : (k + 1) * C] = wt_ref[k * C : (k + 1) * C, :]

    def halo(s, copy, recv, put):
        slot = H + 1 if s == 0 else 0

        @pl.when(has(1 - s))
        def _():
            copy(s).wait_recv()
            each_frame(lambda f: put(f, slot, recv[s, f].astype(F32)))

        @pl.when(jnp.logical_not(has(1 - s)))
        def _():
            each_frame(lambda f: put(f, slot, jnp.zeros((W, C), F32)))

    for h in inner:
        if h == 0:
            halo(1, n_copy, nrecv, put_x)
        if h == H - 1:
            halo(0, n_copy, nrecv, put_x)

        def fn(f, h=h):
            v = dot(xs[f, h], ws_ref[0]) + dot(xs[f, h + 1], ws_ref[1]) + dot(xs[f, h + 2], ws_ref[2])
            hid[f, h] = v
            a = v * jax.nn.sigmoid(v)
            act[f, h] = a.astype(BF16)
            actt[f, h] = a.T.astype(BF16)

        each_frame(fn)

        @pl.when(t < tms - 1)
        def _():
            act_copy(h).start()

    @pl.when(t == tms - 1)
    def _():
        cotn[...] = jnp.zeros_like(cotn)

    def mix(late):
        for h in inner:
            if late:
                act_copy(h).wait_recv()
            acts = [actp[f, h] if late else None for f in range(F)] + [act[f, h] for f in range(F)]
            for f in range(F):
                parts = [a for a in (acts[F + f], acts[F + f - 1], acts[F + f - 2]) if a is not None]
                cc = jnp.concatenate(parts, axis=-1)
                mixed = dot(cc, wt_ref[: len(parts) * C, :])
                out_ref[f, h] = (u_ref[f, h].astype(F32) + mixed).astype(BF16)

    @pl.when(t == 0)
    def _():
        mix(False)

    g32[...] = jnp.zeros_like(g32)
    for h in order:

        @pl.when(t < tms - 1)
        def _():
            cot_copy(h).wait_recv()

        cots = [cot_ref[f, h] for f in range(F)] + [cotn[f, h] for f in range(F)]
        tsum = None
        for f in range(F):
            cc = jnp.concatenate(cots[f : f + 3], axis=-1)
            dact = dot_nt(cc, wtr[...])
            v = hid[f, h]
            s = jax.nn.sigmoid(v)
            dh = (dact * s * (1.0 + v * (1.0 - s))).astype(BF16)
            if h == 0:
                dsend[0, f] = dh
            if h == H - 1:
                dsend[1, f] = dh
            put_d(f, h + 1, dh.astype(F32))
            term = dot(actt[f, h], cc)
            tsum = term if tsum is None else tsum + term
        if h == 0:

            @pl.when(has(0))
            def _():
                d_copy(0).start()

        if h == H - 1:

            @pl.when(has(1))
            def _():
                d_copy(1).start()

        for k in range(3):
            g32[3 * C3 + k * C : 3 * C3 + (k + 1) * C, :] += tsum[:, k * C : (k + 1) * C]
        for i in range(3):
            total = None
            for f in range(F):
                term = dot(xst[f, h + i], d3[f, h + 1, :, C : 2 * C])
                total = term if total is None else total + term
            g32[i * C3 : (i + 1) * C3, :] += total

    g16[...] = g32[...].astype(BF16)
    own = pl.multiple_of(d * half, 16)
    other = pl.multiple_of((1 - d) * half, 16)
    swap = rcopy(g16.at[pl.ds(other, half)], rdp, e1.at[0], e1.at[1], partner)
    swap.start()

    def back(f, h):
        dn = (
            dot_nt(d3[f, h + 2], wsr[0])
            + dot_nt(d3[f, h + 1], wsr[1])
            + dot_nt(d3[f, h], wsr[2])
        )
        r, unit = norm(f, h)
        du = dn * gain
        gin_ref[f, h] = (
            cot_ref[f, h].astype(F32)
            + r * (du - unit * jnp.mean(du * unit, axis=-1, keepdims=True))
        ).astype(BF16)

    swap.wait()
    g32[pl.ds(own, half), :] = g32[pl.ds(own, half), :] + rdp[...].astype(F32)
    s16[...] = g32[pl.ds(own, half), :].astype(BF16)

    def scatter(o):
        q, dev = peer(o)
        return rcopy(
            s16.at[pl.ds(pl.multiple_of(q * ch, 16), ch)],
            rbuf.at[o - 1],
            rss.at[o - 1],
            rrs.at[o - 1],
            dev,
        )

    for o in range(1, n):
        scatter(o).start()

    for h in range(1, H - 1):
        each_frame(functools.partial(back, h=h))

    total = g32[pl.ds(pl.multiple_of(own + p * ch, 8), ch), :]
    for o in range(1, n):
        scatter(o).wait_recv()
        total = total + rbuf[o - 1].astype(F32)

    def place(dd, q):
        return pl.ds(pl.multiple_of((dd * n + q) * ch, 16), ch)

    r16[place(d, p), :] = total.astype(BF16)

    def gather(o):
        return rcopy(r16.at[place(d, p)], r16.at[place(d, p)], gss.at[o - 1], grs.at[o - 1], peer(o)[1])

    def forward(o):
        ref = r16.at[place(d, lax.rem(p - o + n, n))]
        return rcopy(ref, ref, fss.at[o], frs.at[o], partner)

    for o in range(1, n):
        gather(o).start()
    forward(0).start()

    halo(1, d_copy, drecv, put_d)
    each_frame(functools.partial(back, h=0))
    halo(0, d_copy, drecv, put_d)
    each_frame(functools.partial(back, h=H - 1))

    for o in range(1, n):
        gather(o).wait_recv()
        forward(o).start()

    @pl.when(t > 0)
    def _():
        mix(True)

    stores = [
        pltpu.make_async_copy(gin_ref, gin_hbm, osem.at[0]),
        pltpu.make_async_copy(out_ref, out_hbm, osem.at[1]),
    ]
    for store in stores:
        store.start()

    for o in range(n):
        forward(o).wait_recv()
    total = None
    for b in range(9):
        g = r16[b * C : (b + 1) * C, :].astype(F32) * scale
        gs_ref[b] = g
        term = g * ws_ref[b // 3, (b % 3) * C : (b % 3 + 1) * C, :].astype(F32)
        total = term if total is None else total + term
    gg_ref[...] = jnp.sum(total.T, axis=0, keepdims=True) / gain
    for k in range(3):
        gt_ref[k] = r16[(9 + k) * C : (10 + k) * C, :].astype(F32) * scale

    for store in stores:
        store.wait()
    for o in range(1, n):
        scatter(o).wait_send()
        gather(o).wait_send()
    for o in range(n):
        forward(o).wait_send()
    for s in range(2):

        @pl.when(has(s))
        def _():
            n_copy(s).wait_send()
            d_copy(s).wait_send()

    @pl.when(t > 0)
    def _():
        for h in range(H):
            cot_copy(h).wait_send()

    @pl.when(t < tms - 1)
    def _():
        for h in range(H):
            act_copy(h).wait_send()


def settle(*refs):
    count = len(refs) // 2
    sems = refs[-1]
    copies = [
        pltpu.make_async_copy(refs[i], refs[count + i], sems.at[i]) for i in range(count)
    ]
    for copy in copies:
        copy.start()
    for copy in copies:
        copy.wait()


def shards(frames_in, gain, spatial_w, temporal_w, cotangent):
    _, F, H, W, C = frames_in.shape
    rows, tms, dps = lax.axis_size("rows"), lax.axis_size("tm"), lax.axis_size("dp")
    n = rows * tms
    ch = -(-12 * C // (dps * n * 16)) * 16
    total = dps * n * ch
    scale = 1.0 / math.sqrt(F * H * W * n * dps)
    shape = (F, H, W, C)
    vmem = pl.BlockSpec(memory_space=pltpu.VMEM)
    hbm = pl.BlockSpec(memory_space=pl.ANY)
    dma = pltpu.SemaphoreType.DMA
    out = pl.pallas_call(
        functools.partial(kernel, (rows, tms, n, ch), scale),
        out_shape=(
            jax.ShapeDtypeStruct(shape, BF16),
            jax.ShapeDtypeStruct(shape, BF16),
            jax.ShapeDtypeStruct((9, C, C), F32),
            jax.ShapeDtypeStruct((3, C, C), F32),
            jax.ShapeDtypeStruct((1, C), F32),
        ),
        in_specs=[hbm, vmem, hbm, hbm, hbm],
        out_specs=(hbm, hbm, vmem, vmem, vmem),
        scratch_shapes=[
            pltpu.VMEM(shape, BF16),
            pltpu.VMEM((3, 3 * C, C), BF16),
            pltpu.VMEM((3 * C, C), BF16),
            pltpu.VMEM(shape, BF16),
            dma((4,)),
            pltpu.VMEM(shape, BF16),
            pltpu.VMEM(shape, BF16),
            dma((2,)),
            pltpu.VMEM((3, C, 3 * C), BF16),
            pltpu.VMEM((C, 3 * C), BF16),
            pltpu.VMEM((F, H + 2, W, 3 * C), BF16),
            pltpu.VMEM((F, H + 2, 3 * C, W), BF16),
            pltpu.VMEM(shape, F32),
            pltpu.VMEM(shape, BF16),
            pltpu.VMEM((F, H, C, W), BF16),
            pltpu.VMEM((F, H + 2, W, 3 * C), BF16),
            pltpu.VMEM((2, F, W, C), BF16),
            pltpu.VMEM((2, F, W, C), BF16),
            pltpu.VMEM((2, F, W, C), BF16),
            pltpu.VMEM((2, F, W, C), BF16),
            pltpu.VMEM(shape, BF16),
            pltpu.VMEM(shape, BF16),
            pltpu.VMEM((total, C), F32),
            pltpu.VMEM((total, C), BF16),
            pltpu.VMEM((n * ch, C), BF16),
            pltpu.VMEM((n * ch, C), BF16),
            pltpu.VMEM((n - 1, ch, C), BF16),
            pltpu.VMEM((total, C), BF16),
            dma((2,)),
            dma((2,)),
            dma((2,)),
            dma((2,)),
            dma((H,)),
            dma((H,)),
            dma((H,)),
            dma((H,)),
            dma((2,)),
            dma((n - 1,)),
            dma((n - 1,)),
            dma((n - 1,)),
            dma((n - 1,)),
            dma((n,)),
            dma((n,)),
        ],
        compiler_params=pltpu.CompilerParams(
            collective_id=0, has_side_effects=True, vmem_limit_bytes=63 * 1024 * 1024
        ),
    )(
        frames_in.reshape(shape),
        gain.reshape(1, C),
        spatial_w.reshape(3, 3 * C, C),
        temporal_w.reshape(3 * C, C),
        cotangent.reshape(shape),
    )
    anywhere = pl.BlockSpec(memory_space=pl.ANY)
    block_out, grad_input, gs, gt, gg = pl.pallas_call(
        settle,
        out_shape=tuple(jax.ShapeDtypeStruct(o.shape, o.dtype) for o in out),
        in_specs=[vmem] * len(out),
        out_specs=(anywhere,) * len(out),
        scratch_shapes=[dma((len(out),))],
    )(*out)
    return (
        block_out.reshape(frames_in.shape),
        grad_input.reshape(frames_in.shape),
        gs.reshape(3, 3, C, C),
        gt,
        gg.reshape(C),
    )


def solution(mesh):
    split = P(("groups", "dp"), "tm", "rows", None, None)
    return jax.shard_map(
        shards,
        mesh=mesh,
        in_specs=(split, P(), P(), P(), split),
        out_specs=(split, split, P("groups", None, None, None), P("groups", None, None), P("groups")),
        check_vma=False,
    )
```

```python
import functools
import math

import jax
import jax.numpy as jnp
from jax import lax
from jax.experimental import pallas as pl
from jax.experimental.pallas import tpu as pltpu
from jax.sharding import PartitionSpec as P

EPS = 1e-06
MESH = pl.DeviceIdType.MESH
F32 = jnp.float32
BF16 = jnp.bfloat16


def dot(a, b):
    return lax.dot_general(a, b, (((1,), (0,)), ((), ())), preferred_element_type=F32)


def dot_nt(a, b):
    return lax.dot_general(a, b, (((1,), (1,)), ((), ())), preferred_element_type=F32)


def kernel(
    sizes,
    scale,
    u_in,
    gain_ref,
    ws_in,
    wt_in,
    cot_in,
    out_hbm,
    gin_hbm,
    gs_ref,
    gt_ref,
    gg_ref,
    u_ref,
    ws_ref,
    wt_ref,
    cot_ref,
    lsem,
    out_ref,
    gin_ref,
    osem,
    wsr,
    wtr,
    xs,
    xst,
    hid,
    act,
    actt,
    d3,
    nsend,
    nrecv,
    dsend,
    drecv,
    cotn,
    actp,
    g32,
    g16,
    rdp,
    s16,
    rbuf,
    r16,
    nss,
    nrs,
    dss,
    drs,
    css,
    crs,
    ass,
    ars,
    e1,
    rss,
    rrs,
    gss,
    grs,
    fss,
    frs,
):
    rows, tms, n, ch = sizes
    F, H, W, C = u_ref.shape
    loads = [
        pltpu.make_async_copy(a, b, lsem.at[i])
        for i, (a, b) in enumerate(
            ((u_in, u_ref), (ws_in, ws_ref), (cot_in, cot_ref), (wt_in, wt_ref))
        )
    ]
    for load in loads:
        load.start()
    C3 = 3 * C
    half = n * ch
    z = lax.axis_index("rows")
    t = lax.axis_index("tm")
    d = lax.axis_index("dp")
    p = t * rows + z

    def peer(o):
        q = lax.rem(p + o, n)
        return q, {"tm": q // rows, "rows": lax.rem(q, rows)}

    barrier = pltpu.get_barrier_semaphore()
    for o in range(1, n):
        pl.semaphore_signal(barrier, inc=1, device_id=peer(o)[1], device_id_type=MESH)
    partner = {"dp": 1 - d}
    pl.semaphore_signal(barrier, inc=1, device_id=partner, device_id_type=MESH)
    pl.semaphore_wait(barrier, n)

    def rcopy(src, dst, ss, rs, dev):
        return pltpu.make_async_remote_copy(
            src_ref=src, dst_ref=dst, send_sem=ss, recv_sem=rs, device_id=dev, device_id_type=MESH
        )

    order = [0, H - 1] + list(range(1, H - 1))
    inner = list(range(1, H - 1)) + [0, H - 1]

    def cot_copy(h):
        return rcopy(cot_in.at[:, h], cotn.at[:, h], css.at[h], crs.at[h], {"tm": t - 1})

    def act_copy(h):
        return rcopy(act.at[:, h], actp.at[:, h], ass.at[h], ars.at[h], {"tm": t + 1})

    def n_copy(s):
        return rcopy(nsend.at[s], nrecv.at[s], nss.at[s], nrs.at[s], {"rows": z - 1 + 2 * s})

    def d_copy(s):
        return rcopy(dsend.at[s], drecv.at[s], dss.at[s], drs.at[s], {"rows": z - 1 + 2 * s})

    def has(s):
        return z > 0 if s == 0 else z < rows - 1

    @pl.when(t > 0)
    def _():
        for h in order:
            cot_copy(h).start()

    sub = lax.broadcasted_iota(jnp.int32, (W, C), 0)

    def shifted(x):
        before = jnp.where(sub == 0, 0.0, pltpu.roll(x, 1, 0))
        after = jnp.where(sub == W - 1, 0.0, pltpu.roll(x, W - 1, 0))
        return before, after

    def put_x(f, slot, x):
        before, after = shifted(x)
        for j, part in enumerate((before, x, after)):
            xs[f, slot, :, j * C : (j + 1) * C] = part.astype(BF16)
            xst[f, slot, j * C : (j + 1) * C, :] = part.T.astype(BF16)

    def put_d(f, slot, x):
        before, after = shifted(x)
        for j, part in enumerate((after, x, before)):
            d3[f, slot, :, j * C : (j + 1) * C] = part.astype(BF16)

    gain = gain_ref[...]
    loads[0].wait()

    def norm(f, h):
        u = u_ref[f, h].astype(F32)
        r = lax.rsqrt(jnp.mean(u * u, axis=-1, keepdims=True) + EPS)
        return r, u * r

    def each_frame(fn):
        def body(f, carry):
            fn(f)
            return carry

        lax.fori_loop(0, F, body, 0)

    for h in order:

        def fn(f, h=h):
            x = (norm(f, h)[1] * gain).astype(BF16)
            if h == 0:
                nsend[0, f] = x
            if h == H - 1:
                nsend[1, f] = x
            put_x(f, h + 1, x.astype(F32))

        each_frame(fn)
        if h == 0:

            @pl.when(has(0))
            def _():
                n_copy(0).start()

        if h == H - 1:

            @pl.when(has(1))
            def _():
                n_copy(1).start()

    for load in loads[1:]:
        load.wait()
    for i in range(3):
        for j in range(3):
            wsr[i, :, j * C : (j + 1) * C] = ws_ref[i, j * C : (j + 1) * C, :]
    for k in range(3):
        wtr[:, k * C : (k + 1) * C] = wt_ref[k * C : (k + 1) * C, :]

    def halo(s, copy, recv, put):
        slot = H + 1 if s == 0 else 0

        @pl.when(has(1 - s))
        def _():
            copy(s).wait_recv()
            each_frame(lambda f: put(f, slot, recv[s, f].astype(F32)))

        @pl.when(jnp.logical_not(has(1 - s)))
        def _():
            each_frame(lambda f: put(f, slot, jnp.zeros((W, C), F32)))

    for h in inner:
        if h == 0:
            halo(1, n_copy, nrecv, put_x)
        if h == H - 1:
            halo(0, n_copy, nrecv, put_x)

        def fn(f, h=h):
            v = dot(xs[f, h], ws_ref[0]) + dot(xs[f, h + 1], ws_ref[1]) + dot(xs[f, h + 2], ws_ref[2])
            hid[f, h] = v
            a = v * jax.nn.sigmoid(v)
            act[f, h] = a.astype(BF16)
            actt[f, h] = a.T.astype(BF16)

        each_frame(fn)

        @pl.when(t < tms - 1)
        def _():
            act_copy(h).start()

    @pl.when(t == tms - 1)
    def _():
        cotn[...] = jnp.zeros_like(cotn)

    def mix(late):
        for h in inner:
            if late:
                act_copy(h).wait_recv()
            acts = [actp[f, h] if late else None for f in range(F)] + [act[f, h] for f in range(F)]
            for f in range(F):
                parts = [a for a in (acts[F + f], acts[F + f - 1], acts[F + f - 2]) if a is not None]
                cc = jnp.concatenate(parts, axis=-1)
                mixed = dot(cc, wt_ref[: len(parts) * C, :])
                out_ref[f, h] = (u_ref[f, h].astype(F32) + mixed).astype(BF16)

    @pl.when(t == 0)
    def _():
        mix(False)

    g32[...] = jnp.zeros_like(g32)
    for h in order:

        @pl.when(t < tms - 1)
        def _():
            cot_copy(h).wait_recv()

        cots = [cot_ref[f, h] for f in range(F)] + [cotn[f, h] for f in range(F)]
        tsum = None
        for f in range(F):
            cc = jnp.concatenate(cots[f : f + 3], axis=-1)
            dact = dot_nt(cc, wtr[...])
            v = hid[f, h]
            s = jax.nn.sigmoid(v)
            dh = (dact * s * (1.0 + v * (1.0 - s))).astype(BF16)
            if h == 0:
                dsend[0, f] = dh
            if h == H - 1:
                dsend[1, f] = dh
            put_d(f, h + 1, dh.astype(F32))
            term = dot(actt[f, h], cc)
            tsum = term if tsum is None else tsum + term
        if h == 0:

            @pl.when(has(0))
            def _():
                d_copy(0).start()

        if h == H - 1:

            @pl.when(has(1))
            def _():
                d_copy(1).start()

        for k in range(3):
            g32[3 * C3 + k * C : 3 * C3 + (k + 1) * C, :] += tsum[:, k * C : (k + 1) * C]
        for i in range(3):
            total = None
            for f in range(F):
                term = dot(xst[f, h + i], d3[f, h + 1, :, C : 2 * C])
                total = term if total is None else total + term
            g32[i * C3 : (i + 1) * C3, :] += total

    g16[...] = g32[...].astype(BF16)
    own = pl.multiple_of(d * half, 16)
    other = pl.multiple_of((1 - d) * half, 16)
    swap = rcopy(g16.at[pl.ds(other, half)], rdp, e1.at[0], e1.at[1], partner)
    swap.start()

    def back(f, h):
        dn = (
            dot_nt(d3[f, h + 2], wsr[0])
            + dot_nt(d3[f, h + 1], wsr[1])
            + dot_nt(d3[f, h], wsr[2])
        )
        r, unit = norm(f, h)
        du = dn * gain
        gin_ref[f, h] = (
            cot_ref[f, h].astype(F32)
            + r * (du - unit * jnp.mean(du * unit, axis=-1, keepdims=True))
        ).astype(BF16)

    each_frame(functools.partial(back, h=1))
    swap.wait()
    g32[pl.ds(own, half), :] = g32[pl.ds(own, half), :] + rdp[...].astype(F32)
    s16[...] = g32[pl.ds(own, half), :].astype(BF16)

    def scatter(o):
        q, dev = peer(o)
        return rcopy(
            s16.at[pl.ds(pl.multiple_of(q * ch, 16), ch)],
            rbuf.at[o - 1],
            rss.at[o - 1],
            rrs.at[o - 1],
            dev,
        )

    for o in range(1, n):
        scatter(o).start()

    for h in range(2, H - 1):
        each_frame(functools.partial(back, h=h))

    total = g32[pl.ds(pl.multiple_of(own + p * ch, 8), ch), :]
    for o in range(1, n):
        scatter(o).wait_recv()
        total = total + rbuf[o - 1].astype(F32)

    def place(dd, q):
        return pl.ds(pl.multiple_of((dd * n + q) * ch, 16), ch)

    r16[place(d, p), :] = total.astype(BF16)

    def gather(o):
        return rcopy(r16.at[place(d, p)], r16.at[place(d, p)], gss.at[o - 1], grs.at[o - 1], peer(o)[1])

    def forward(o):
        ref = r16.at[place(d, lax.rem(p - o + n, n))]
        return rcopy(ref, ref, fss.at[o], frs.at[o], partner)

    for o in range(1, n):
        gather(o).start()
    forward(0).start()

    halo(1, d_copy, drecv, put_d)
    each_frame(functools.partial(back, h=0))
    halo(0, d_copy, drecv, put_d)
    each_frame(functools.partial(back, h=H - 1))

    for o in range(1, n):
        gather(o).wait_recv()
        forward(o).start()

    @pl.when(t > 0)
    def _():
        mix(True)

    stores = [
        pltpu.make_async_copy(gin_ref, gin_hbm, osem.at[0]),
        pltpu.make_async_copy(out_ref, out_hbm, osem.at[1]),
    ]
    for store in stores:
        store.start()

    for o in range(n):
        forward(o).wait_recv()
    total = None
    for b in range(9):
        g = r16[b * C : (b + 1) * C, :].astype(F32) * scale
        gs_ref[b] = g
        term = g * ws_ref[b // 3, (b % 3) * C : (b % 3 + 1) * C, :].astype(F32)
        total = term if total is None else total + term
    gg_ref[...] = jnp.sum(total.T, axis=0, keepdims=True) / gain
    for k in range(3):
        gt_ref[k] = r16[(9 + k) * C : (10 + k) * C, :].astype(F32) * scale

    for store in stores:
        store.wait()
    for o in range(1, n):
        scatter(o).wait_send()
        gather(o).wait_send()
    for o in range(n):
        forward(o).wait_send()
    for s in range(2):

        @pl.when(has(s))
        def _():
            n_copy(s).wait_send()
            d_copy(s).wait_send()

    @pl.when(t > 0)
    def _():
        for h in range(H):
            cot_copy(h).wait_send()

    @pl.when(t < tms - 1)
    def _():
        for h in range(H):
            act_copy(h).wait_send()


def settle(*refs):
    count = len(refs) // 2
    sems = refs[-1]
    copies = [
        pltpu.make_async_copy(refs[i], refs[count + i], sems.at[i]) for i in range(count)
    ]
    for copy in copies:
        copy.start()
    for copy in copies:
        copy.wait()


def shards(frames_in, gain, spatial_w, temporal_w, cotangent):
    _, F, H, W, C = frames_in.shape
    rows, tms, dps = lax.axis_size("rows"), lax.axis_size("tm"), lax.axis_size("dp")
    n = rows * tms
    ch = -(-12 * C // (dps * n * 16)) * 16
    total = dps * n * ch
    scale = 1.0 / math.sqrt(F * H * W * n * dps)
    shape = (F, H, W, C)
    vmem = pl.BlockSpec(memory_space=pltpu.VMEM)
    hbm = pl.BlockSpec(memory_space=pl.ANY)
    dma = pltpu.SemaphoreType.DMA
    out = pl.pallas_call(
        functools.partial(kernel, (rows, tms, n, ch), scale),
        out_shape=(
            jax.ShapeDtypeStruct(shape, BF16),
            jax.ShapeDtypeStruct(shape, BF16),
            jax.ShapeDtypeStruct((9, C, C), F32),
            jax.ShapeDtypeStruct((3, C, C), F32),
            jax.ShapeDtypeStruct((1, C), F32),
        ),
        in_specs=[hbm, vmem, hbm, hbm, hbm],
        out_specs=(hbm, hbm, vmem, vmem, vmem),
        scratch_shapes=[
            pltpu.VMEM(shape, BF16),
            pltpu.VMEM((3, 3 * C, C), BF16),
            pltpu.VMEM((3 * C, C), BF16),
            pltpu.VMEM(shape, BF16),
            dma((4,)),
            pltpu.VMEM(shape, BF16),
            pltpu.VMEM(shape, BF16),
            dma((2,)),
            pltpu.VMEM((3, C, 3 * C), BF16),
            pltpu.VMEM((C, 3 * C), BF16),
            pltpu.VMEM((F, H + 2, W, 3 * C), BF16),
            pltpu.VMEM((F, H + 2, 3 * C, W), BF16),
            pltpu.VMEM(shape, F32),
            pltpu.VMEM(shape, BF16),
            pltpu.VMEM((F, H, C, W), BF16),
            pltpu.VMEM((F, H + 2, W, 3 * C), BF16),
            pltpu.VMEM((2, F, W, C), BF16),
            pltpu.VMEM((2, F, W, C), BF16),
            pltpu.VMEM((2, F, W, C), BF16),
            pltpu.VMEM((2, F, W, C), BF16),
            pltpu.VMEM(shape, BF16),
            pltpu.VMEM(shape, BF16),
            pltpu.VMEM((total, C), F32),
            pltpu.VMEM((total, C), BF16),
            pltpu.VMEM((n * ch, C), BF16),
            pltpu.VMEM((n * ch, C), BF16),
            pltpu.VMEM((n - 1, ch, C), BF16),
            pltpu.VMEM((total, C), BF16),
            dma((2,)),
            dma((2,)),
            dma((2,)),
            dma((2,)),
            dma((H,)),
            dma((H,)),
            dma((H,)),
            dma((H,)),
            dma((2,)),
            dma((n - 1,)),
            dma((n - 1,)),
            dma((n - 1,)),
            dma((n - 1,)),
            dma((n,)),
            dma((n,)),
        ],
        compiler_params=pltpu.CompilerParams(
            collective_id=0, has_side_effects=True, vmem_limit_bytes=63 * 1024 * 1024
        ),
    )(
        frames_in.reshape(shape),
        gain.reshape(1, C),
        spatial_w.reshape(3, 3 * C, C),
        temporal_w.reshape(3 * C, C),
        cotangent.reshape(shape),
    )
    anywhere = pl.BlockSpec(memory_space=pl.ANY)
    block_out, grad_input, gs, gt, gg = pl.pallas_call(
        settle,
        out_shape=tuple(jax.ShapeDtypeStruct(o.shape, o.dtype) for o in out),
        in_specs=[vmem] * len(out),
        out_specs=(anywhere,) * len(out),
        scratch_shapes=[dma((len(out),))],
    )(*out)
    return (
        block_out.reshape(frames_in.shape),
        grad_input.reshape(frames_in.shape),
        gs.reshape(3, 3, C, C),
        gt,
        gg.reshape(C),
    )


def solution(mesh):
    split = P(("groups", "dp"), "tm", "rows", None, None)
    return jax.shard_map(
        shards,
        mesh=mesh,
        in_specs=(split, P(), P(), P(), split),
        out_specs=(split, split, P("groups", None, None, None), P("groups", None, None), P("groups")),
        check_vma=False,
    )
```
